512 devices in a mesh: train: 16 (over x, z_hi, core), roll: 32 (over z_lo, y).
Axes of the slice: x: 4, y: 8, z: 8 (z_hi: 2, z_lo: 4; z = z_hi * 4 + z_lo), core: 2. Of those that a mesh axis runs over, the one named last changes fastest.
Arguments:
- hidden: bfloat16 [24576, 8192], P(('train', 'roll')), may hold values from -6 to 6
- ssm_state: bfloat16 [24576, 1, 64, 256], P(('train', 'roll')), may hold values from -6 to 6
- conv_state: bfloat16 [24576, 3, 576], P(('train', 'roll')), may hold values from -6 to 6
- lengths: int32 [24576], P(('train', 'roll')), may hold values from 1 to 8
- dest_owner: int32 [24576], P(('train', 'roll')), may hold values from 0 to 31, as said below
- dest_slot: int32 [24576], P(('train', 'roll')), may hold values from 0 to 47, as said below
- weights_in: bfloat16 [8192, 640], P('train'), may hold values from -0.0625 to 0.0625
- weights_dt: bfloat16 [8192, 1], P('train'), may hold values from -0.0625 to 0.0625
- weights_out: bfloat16 [64, 8192], P(None, 'train'), may hold values from -0.75 to 0.75
- input_gain: float32 [8192], replicated, may hold values from 0.5 to 1.5
- conv_weight: float32 [4, 576], replicated, may hold values from -3 to 3
- conv_bias: float32 [576], replicated, may hold values from -3 to 3
- delta_bias: float32 [1], replicated, may hold values from -3 to 1
- decay_log: float32 [1], replicated, may hold values from -1 to 1.5
- skip_gain: float32 [1], replicated, may hold values from 0.5 to 1.5
- output_gain: float32 [64], replicated, may hold values from 0.5 to 1.5
Outputs:
- moved_state: bfloat16 [24576, 1, 64, 256], P(('train', 'roll'))
- moved_conv: bfloat16 [24576, 3, 576], P(('train', 'roll'))
The draws below stay inside these ranges and needn't reach their ends.
Inputs may be any that keep to these rules, and one draw needn't show every extreme that they name: `dest_owner`: within one train index, each row names a roll index as its new owner. A device sends at most 2 rows to one owner, and exactly 2 to some owner. `dest_slot`: within one train index, each owner's 48 slots are each named by exactly one row.
All inputs are finite; a program needn't handle non-finite values.
Results may differ from the reference program's by a relative error of at most 0.015.
Values may be sent and summed in bfloat16 or wider, within the bound.
No kernel may reach another device: no remote copies, remote signals or barrier semaphores. Data moves between devices by JAX's collectives and lax.ppermute only.
A program may use at most 64 MiB of HBM per device.

```python
import jax
import jax.numpy as jnp
from jax import lax

D = 8192
HD = 64
NS = 256
KC = 4
HW = 1
STEPS = 4
ROWS_DEV = 48
INNER = 64
CONV = 576
IN_COLS = 640
CAP = 2
ROWS = 24576
N_TRAIN = 16
N_ROLL = 32


def route_tables(key):

    def one_group(group_key):
        key_values, key_order, key_rows = jax.random.split(group_key, 3)
        values = jax.random.permutation(key_values, N_ROLL)
        offsets = values[jnp.arange(ROWS_DEV) // CAP]
        offsets = jax.random.permutation(key_order, offsets)

        def one_source(source_key, source):
            slots = jax.random.permutation(source_key, ROWS_DEV)
            owners = (source + offsets[slots]) % N_ROLL
            return (owners, slots)
        source_keys = jax.random.split(key_rows, N_ROLL)
        owners, slots = jax.vmap(one_source)(source_keys, jnp.arange(N_ROLL))
        return (owners.reshape(-1), slots.reshape(-1))
    group_keys = jax.random.split(key, N_TRAIN)
    owners, slots = jax.vmap(one_group)(group_keys)
    return (owners.reshape(-1).astype(jnp.int32), slots.reshape(-1).astype(jnp.int32))


def draw_dest_owner(key, part):
    tables = route_tables(key)
    return tables[0]


def draw_dest_slot(key, part):
    tables = route_tables(key)
    return tables[1]


def plant(array, rng, low, largest):
    shape = array.shape
    spot = [jax.random.randint(jax.random.fold_in(rng, axis), (), 0, shape[axis]) for axis in range(len(shape))]
    array = array.at[tuple(spot)].set(low)
    longest = shape.index(max(shape))
    spot[longest] = (spot[longest] + 1) % shape[longest]
    return array.at[tuple(spot)].set(largest)


def level_of(rng, extent, cuts, smallest, top_value):
    def one(axis_at, shards_of):
        draws = jax.random.uniform(jax.random.fold_in(jax.random.fold_in(rng, 6), axis_at), (shards_of,), jnp.float32, smallest / len(cuts), top_value / len(cuts))
        return jnp.repeat(jnp.exp(draws), extent[axis_at] // shards_of).reshape((-1,) + (1,) * (len(extent) - axis_at - 1))

    level = one(*cuts[0])
    for cut in cuts[1:]:
        level = level * one(*cut)
    return level


def normal_values(key, dims, spread, most, cuts=(), held_as=jnp.bfloat16):
    entries = spread * jax.random.normal(key, dims, jnp.float32)
    if cuts:
        entries = entries * level_of(key, dims, cuts, -0.22, 0.18)
    return jnp.clip(entries, -most, most).astype(held_as)


def setup_inputs(seed: int = 0) -> dict:
    key_list = jax.random.split(jax.random.key(seed), 17)
    return {
        "hidden": normal_values(key_list[0], (ROWS, D), 1.0, 6.0, ((0, 512),)),
        "ssm_state": normal_values(key_list[1], (ROWS, HW, HD, NS), 1.0, 6.0, ((0, 512),)),
        "conv_state": normal_values(key_list[2], (ROWS, KC - 1, CONV), 1.0, 6.0, ((0, 512),)),
        "lengths": plant(jax.random.randint(key_list[3], (ROWS,), 1, 2 * STEPS + 1), jax.random.fold_in(key_list[3], 1), 1, 2 * STEPS).astype(jnp.int32),
        "dest_owner": draw_dest_owner(jax.random.fold_in(key_list[16], 71), 0),
        "dest_slot": draw_dest_slot(jax.random.fold_in(key_list[16], 71), 0),
        "weights_in": normal_values(key_list[6], (D, IN_COLS), D ** -0.5, 0.0625, ((0, 16),)),
        "weights_dt": normal_values(key_list[7], (D, HW), D ** -0.5, 0.0625, ((0, 16),)),
        "weights_out": normal_values(key_list[8], (INNER, D), INNER ** -0.5, 0.75, ((1, 16),)),
        "input_gain": jnp.clip(1.0 + 0.1 * jax.random.normal(key_list[9], (D,), jnp.float32), 0.5, 1.5),
        "conv_weight": normal_values(key_list[10], (KC, CONV), KC ** -0.5, 3.0, (), jnp.float32),
        "conv_bias": normal_values(key_list[11], (CONV,), 0.5, 3.0, (), jnp.float32),
        "delta_bias": jnp.clip(jax.random.uniform(key_list[12], (HW,), jnp.float32, -3.0, 1.0), -3.0, 1.0),
        "decay_log": jnp.clip(jax.random.uniform(key_list[13], (HW,), jnp.float32, -1.0, 1.5), -1.0, 1.5),
        "skip_gain": jnp.clip(jax.random.uniform(key_list[14], (HW,), jnp.float32, 0.5, 1.5), 0.5, 1.5),
        "output_gain": jnp.clip(1.0 + 0.1 * jax.random.normal(key_list[15], (INNER,), jnp.float32), 0.5, 1.5),
    }


def rms_scale(values, gain):
    return values * lax.rsqrt(lax.optimization_barrier(jnp.mean(values * values, axis=-1, keepdims=True)) + 1e-05) * gain

def decode_steps(hidden, ssm_state, conv_state, lengths, weights_in, weights_dt, weights_out, input_gain, conv_weight, conv_bias, delta_bias, decay_log, skip_gain, output_gain):
    inner = weights_out.shape[0]
    heads = delta_bias.shape[0]
    head_size = inner // heads
    nstate = ssm_state.shape[-1]
    count = hidden.shape[0]
    for step in range(STEPS):
        live = lengths > step
        current = hidden.astype(jnp.float32)
        normed = rms_scale(current, input_gain).astype(jnp.bfloat16)
        projected = jnp.dot(normed, weights_in, preferred_element_type=jnp.float32)
        delta_raw = jnp.dot(normed, weights_dt, preferred_element_type=jnp.float32)
        gate_part = projected[:, :inner]
        conv_input = projected[:, inner:].astype(jnp.bfloat16)
        window = jnp.concatenate([conv_state, conv_input[:, None, :]], axis=1)
        mixed = jax.nn.silu(lax.optimization_barrier(jnp.sum(window.astype(jnp.float32) * conv_weight[None], axis=1)) + conv_bias)
        inputs_x = mixed[:, :inner].reshape(count, heads, head_size)
        input_b = mixed[:, inner:inner + nstate]
        output_c = mixed[:, inner + nstate:]
        delta = jax.nn.softplus(delta_raw + delta_bias)
        decay = jnp.exp(-delta * jnp.exp(decay_log))
        updated = ssm_state.astype(jnp.float32) * decay[:, :, None, None] + (delta[:, :, None] * inputs_x)[:, :, :, None] * input_b[:, None, None, :]
        readout = lax.optimization_barrier(jnp.sum(updated * output_c[:, None, None, :], axis=-1)) + skip_gain[None, :, None] * inputs_x
        gated = readout.reshape(count, inner) * jax.nn.silu(gate_part)
        normed_out = rms_scale(gated, output_gain).astype(jnp.bfloat16)
        layer_out = jnp.dot(normed_out, weights_out, preferred_element_type=jnp.float32)
        next_hidden = (current + layer_out).astype(jnp.bfloat16)
        ssm_state = jnp.where(live[:, None, None, None], updated.astype(jnp.bfloat16), ssm_state)
        conv_state = jnp.where(live[:, None, None], window[:, 1:], conv_state)
        hidden = jnp.where(live[:, None], next_hidden, hidden)
    return (ssm_state, conv_state)

def reference(hidden, ssm_state, conv_state, lengths, dest_owner, dest_slot, weights_in, weights_dt, weights_out, input_gain, conv_weight, conv_bias, delta_bias, decay_log, skip_gain, output_gain):
    group_rows = N_ROLL * ROWS_DEV

    def one_group(pieces):
        group_hidden, group_state, group_conv, group_lengths, group_owner, group_slot = pieces
        new_state, new_conv = decode_steps(group_hidden, group_state, group_conv, group_lengths, weights_in, weights_dt, weights_out, input_gain, conv_weight, conv_bias, delta_bias, decay_log, skip_gain, output_gain)
        unfinished = group_lengths > STEPS
        target = (group_owner * ROWS_DEV + group_slot).astype(jnp.int32)
        kept_state = jnp.where(unfinished[:, None, None, None], new_state, jnp.zeros_like(new_state))
        kept_conv = jnp.where(unfinished[:, None, None], new_conv, jnp.zeros_like(new_conv))
        placed_state = jnp.zeros_like(new_state).at[target].set(kept_state)
        placed_conv = jnp.zeros_like(new_conv).at[target].set(kept_conv)
        return (placed_state, placed_conv)
    stacked = (hidden.reshape(N_TRAIN, group_rows, D), ssm_state.reshape(N_TRAIN, group_rows, HW, HD, NS), conv_state.reshape(N_TRAIN, group_rows, KC - 1, CONV), lengths.reshape(N_TRAIN, group_rows), dest_owner.reshape(N_TRAIN, group_rows), dest_slot.reshape(N_TRAIN, group_rows))
    placed_state, placed_conv = lax.map(one_group, stacked)
    return (placed_state.reshape(ROWS, HW, HD, NS), placed_conv.reshape(ROWS, KC - 1, CONV))
```

```python
import functools

import jax
import jax.numpy as jnp
from jax import lax
from jax.experimental import pallas as pl
from jax.experimental.pallas import tpu as pltpu
from jax.sharding import PartitionSpec as P

STEPS = 4
CAP = 2
ROWS = 48
HEAD = 64
NS = 256
CONV = 576
WIDTH = 8192
NX = 4
NZ = 4
NY = 8
N_ROLL = NZ * NY
BLOCK = 512
SPAN = 4 * BLOCK
COLS = 768
GATE = CONV
BACK = GATE + HEAD
STEP = BACK + HEAD
LATE = NS + CONV + HEAD
F32 = jnp.float32
BF16 = jnp.bfloat16
VMEM = pl.BlockSpec(memory_space=pltpu.VMEM)
SMEM = pl.BlockSpec(memory_space=pltpu.SMEM)
HBM = pl.BlockSpec(memory_space=pltpu.HBM)


def prepare_kernel(
    owner_ref,
    state_ref,
    hidden_ref,
    gain_ref,
    in_ref,
    dt_ref,
    out_ref,
    send_ref,
    place_ref,
    weights_ref,
    square_ref,
    h0,
    h1,
    h2,
    h3,
    count_ref,
    states,
    rows,
    load_sem,
    state_sem,
    span_sem,
):
    train = lax.axis_index("train")
    load_rows = pltpu.make_async_copy(hidden_ref, rows, load_sem.at[0])
    load_rows.start()
    load_states = pltpu.make_async_copy(state_ref, states, load_sem.at[1])
    load_states.start()

    weights_ref[:, : 2 * NS] = in_ref[:, 2 * HEAD :]
    rest = in_ref[:, : 2 * HEAD].astype(F32)
    weights_ref[:, 2 * NS : BACK] = jnp.concatenate([rest[:, HEAD:], rest[:, :HEAD]], axis=1).astype(BF16)
    steps = jnp.concatenate([dt_ref[...].astype(F32), jnp.zeros((HEAD - 1, BLOCK), F32)], axis=0)
    weights_ref[:, BACK:] = jnp.concatenate([out_ref[...].astype(F32), steps], axis=0).T.astype(BF16)

    load_rows.wait()
    square = jnp.zeros((ROWS, 1), F32)
    for b in range(WIDTH // BLOCK):
        some = rows[:, b * BLOCK : (b + 1) * BLOCK].astype(F32)
        square = square + jnp.sum(some * some, axis=1, keepdims=True)
    square_ref[...] = square
    scale = lax.rsqrt(square * (1.0 / WIDTH) + 1e-05)
    for b in range(WIDTH // BLOCK):
        cols = slice(b * BLOCK, (b + 1) * BLOCK)
        rows[:, cols] = (rows[:, cols].astype(F32) * scale * gain_ref[cols].reshape(1, BLOCK)).astype(BF16)
    spans = []
    for k, ref in enumerate((h0, h1, h2, h3)):
        for b in range(4):
            block = lax.rem(train // 4 + k, NX) * 4 + (lax.rem(train, 4) ^ b)
            spans.append(
                pltpu.make_async_copy(
                    rows.at[:, pl.ds(pl.multiple_of(block * BLOCK, BLOCK), BLOCK)],
                    ref.at[:, pl.ds(b * BLOCK, BLOCK)],
                    span_sem.at[4 * k + b],
                )
            )
            spans[-1].start()
    load_states.wait()
    for o in range(N_ROLL):
        count_ref[o] = 0
    for i in range(ROWS):
        o = owner_ref[i]
        rank = count_ref[o]
        count_ref[o] = rank + 1
        place = o * CAP + rank
        place_ref[i] = place
        pltpu.make_async_copy(states.at[i], send_ref.at[place], state_sem).start()
    pltpu.make_async_copy(states, send_ref.at[pl.ds(0, ROWS)], state_sem).wait()
    for copy in spans:
        copy.wait()


def project_kernel(gain_ref, h0, h1, h2, h3, w0, w1, w2, w3, own_ref, p1, p2, p3):
    count = NX * ROWS
    total, backs = None, None
    for b, w in enumerate((w0, w1, w2, w3)):
        gain = gain_ref[b : b + 1]
        weights = w[...]
        back = weights[:, BACK:].T[:HEAD]
        gained = back.astype(F32) * gain
        high = gained.astype(BF16)
        low = (gained - high.astype(F32)).astype(BF16)
        normed = jnp.concatenate([h[:, b * BLOCK : (b + 1) * BLOCK] for h in (h0, h1, h2, h3)], axis=0)
        left = jnp.concatenate([normed, high, low], axis=0)
        part = jnp.dot(left, weights, preferred_element_type=F32)
        bare = (normed.astype(F32) * (1.0 / gain)).astype(BF16)
        left = jnp.concatenate([bare, back], axis=0)
        part_back = jnp.dot(left, weights[:, BACK:], preferred_element_type=F32)
        total = part if total is None else total + part
        backs = part_back if backs is None else backs + part_back
    total = jnp.concatenate([total[:count], total[count : count + HEAD] + total[count + HEAD :]], axis=0)
    lane = lax.broadcasted_iota(jnp.int32, backs.shape, 1)
    last = jnp.where(lane < HEAD, backs, total[:, BACK:])
    total = jnp.concatenate([total[:, :BACK], last], axis=1)
    grow = total[count:]
    own_ref[:ROWS] = total[:ROWS]
    own_ref[ROWS:] = grow
    grow_high = grow.astype(BF16)
    grow_low = (grow - grow_high.astype(F32)).astype(BF16)
    for k, ref in enumerate((p1, p2, p3)):
        rows = total[(k + 1) * ROWS : (k + 2) * ROWS]
        high = rows.astype(BF16)
        ref[:ROWS] = high
        ref[ROWS : 2 * ROWS] = (rows - high.astype(F32)).astype(BF16)
        ref[2 * ROWS : 2 * ROWS + HEAD] = grow_high
        ref[2 * ROWS + HEAD :] = grow_low


def silu(v):
    return v * jax.nn.sigmoid(v)


def decode_kernel(
    scalar_ref,
    own,
    r1,
    r2,
    r3,
    square_ref,
    state_hbm,
    conv,
    taps,
    bias,
    gain,
    code,
    placeq,
    out,
    state,
    packed,
    state_sem,
):
    load = pltpu.make_async_copy(state_hbm, state, state_sem)
    load.start()
    square = square_ref[...]
    first, grow = own[:ROWS], own[ROWS:]
    for r in (r1, r2, r3):
        first = first + (r[:ROWS].astype(F32) + r[ROWS : 2 * ROWS].astype(F32))
        grow = grow + (r[2 * ROWS : 2 * ROWS + HEAD].astype(F32) + r[2 * ROWS + HEAD :].astype(F32))
    high = grow.astype(BF16)
    grow = jnp.concatenate([high, (grow - high.astype(F32)).astype(BF16)], axis=0)
    raw = first * jnp.sqrt(square * (1.0 / WIDTH) + 1e-05)
    delta_bias, rate, skip = scalar_ref[0], jnp.exp(jnp.full((1, 1), scalar_ref[1], F32)), scalar_ref[2]
    window = [conv[k].astype(F32) for k in range(3)]
    product = jnp.ones((ROWS, 1), F32)
    scaled, inputs_b, entered = [], [], []
    row8 = lax.broadcasted_iota(jnp.int32, (8, HEAD), 0)
    for step in range(STEPS):
        if step == 0:
            projected = first
        else:
            projected = raw * lax.rsqrt(square * (1.0 / WIDTH) + 1e-05)
        conv_input = projected[:, :CONV].astype(BF16).astype(F32)
        window.append(conv_input)
        entered.append(conv_input)
        mixed = bias[...]
        for k in range(4):
            mixed = mixed + window[step + k] * taps[k : k + 1]
        mixed = silu(mixed)
        input_b, output_c, inputs_x = mixed[:, :NS], mixed[:, NS : 2 * NS], mixed[:, 2 * NS :]
        delta = jax.nn.softplus(projected[:, STEP : STEP + 1] + delta_bias)
        decay = jnp.exp(-delta * rate)
        product = product * decay
        scaled = [u * decay for u in scaled] + [delta * inputs_x]
        inputs_b.append(input_b)
        if step == STEPS - 1:
            break
        high = output_c.astype(BF16)
        low = (output_c - high.astype(F32)).astype(BF16)
        if step == 0:
            load.wait()
        reads = []
        for g in range(ROWS // 8):
            left = jnp.concatenate([high[8 * g : 8 * g + 8], low[8 * g : 8 * g + 8]], axis=0)
            acc = jnp.zeros((8, HEAD), F32)
            for half in range(2):
                four = state[8 * g + 4 * half : 8 * g + 4 * half + 4].reshape(4 * HEAD, NS)
                both = lax.dot_general(left, four, (((1,), (1,)), ((), ())), preferred_element_type=F32)
                both = both[:8] + both[8:]
                for i in range(4):
                    acc = jnp.where(row8 == 4 * half + i, both[:, HEAD * i : HEAD * (i + 1)], acc)
            reads.append(acc)
        readout = product * jnp.concatenate(reads, axis=0) + skip * inputs_x
        for u, b in zip(scaled, inputs_b):
            readout = readout + u * jnp.sum(b * output_c, axis=1, keepdims=True)
        gated = readout * silu(projected[:, GATE : GATE + HEAD])
        mean = jnp.mean(gated * gated, axis=1, keepdims=True)
        normed_out = (gated * lax.rsqrt(mean + 1e-05) * gain[...]).astype(BF16)
        twice = jnp.concatenate([normed_out, normed_out], axis=1)
        after = raw + jnp.dot(twice, grow, preferred_element_type=F32)
        cross = raw[:, BACK : BACK + HEAD] + after[:, BACK : BACK + HEAD]
        square = jnp.maximum(
            square + jnp.sum(normed_out.astype(F32) * cross, axis=1, keepdims=True), 0.0
        )
        raw = after
    lane = lax.broadcasted_iota(jnp.int32, (ROWS, CONV), 1)
    high = product.astype(BF16).astype(F32)
    entered[0] = jnp.where(
        lane == 0, code[...], jnp.where(lane == 1, high, jnp.where(lane == 2, product - high, 0.0))
    )
    for step in range(STEPS):
        packed[step * ROWS : (step + 1) * ROWS] = jnp.concatenate(
            [inputs_b[step], entered[step], scaled[step]], axis=1
        ).astype(BF16)
    picker = (
        lax.broadcasted_iota(jnp.int32, (N_ROLL * CAP * STEPS, STEPS * ROWS), 0) == placeq[...]
    ).astype(F32).astype(BF16)
    out[...] = jnp.dot(picker, packed[...], preferred_element_type=F32).astype(BF16)


def after_kernel(late, arrived, out):
    pass


def combine_kernel(
    state_hbm,
    late,
    out_hbm,
    out_conv,
    state,
    out_state,
    rows_ref,
    codes_ref,
    index_ref,
    where_ref,
    sem,
    load_sem,
    store_sem,
):
    load = pltpu.make_async_copy(state_hbm, state, load_sem)
    load.start()
    slots = N_ROLL * CAP
    pick = (lax.broadcasted_iota(jnp.int32, (8, 128), 1) == 0).astype(F32).astype(BF16)
    codes = lax.dot_general(
        pick, late[:, NS : NS + 128], (((1,), (1,)), ((), ())), preferred_element_type=F32
    ).astype(jnp.int32)
    column = lax.broadcasted_iota(jnp.int32, (8, slots * STEPS), 1)
    step_of = column % STEPS
    codes = jnp.where(step_of == 0, codes, 0)
    codes_ref[...] = codes
    copy = pltpu.make_async_copy(codes_ref, index_ref, sem)
    copy.start()
    for step in range(1, STEPS):
        codes = jnp.where(step_of == step, pltpu.roll(codes, 1, axis=1), codes)

    def spread(rows, wanted):
        return (lax.broadcasted_iota(jnp.int32, (rows, slots * STEPS), 0) == wanted[:1]).astype(F32).astype(BF16)

    by_row = jnp.where(codes > 0, (codes - 1) * STEPS + step_of, -1)
    by_step = jnp.where((codes > 0) & (step_of > 0), (step_of - 1) * ROWS + codes - 1, -1)
    rows_ref[...] = jnp.dot(spread(STEPS * ROWS, by_row), late[...], preferred_element_type=F32)
    entered = jnp.dot(
        spread((STEPS - 1) * ROWS, by_step), late[:, NS : NS + CONV], preferred_element_type=F32
    )
    entered = jnp.concatenate([entered[:, 2 * NS :], entered[:, : 2 * NS]], axis=1).astype(BF16)
    for step in range(STEPS - 1):
        out_conv[step] = entered[step * ROWS : (step + 1) * ROWS]
    copy.wait()
    for s in range(ROWS + 1):
        where_ref[s] = -1
    for k in range(slots):
        where_ref[index_ref[0, k * STEPS]] = k

    load.wait()
    stores = []
    group = 4
    lanes = group * HEAD
    some = group * STEPS
    mine = (
        lax.broadcasted_iota(jnp.int32, (some, lanes), 0) // STEPS
        == lax.broadcasted_iota(jnp.int32, (some, lanes), 1) // HEAD
    )
    for g in range(ROWS // group):
        rows = rows_ref[some * g : some * (g + 1)]
        scaled = rows[:, NS + CONV :]
        scaled = jnp.where(mine, jnp.concatenate([scaled] * group, axis=1), 0.0).astype(BF16)
        outer = lax.dot_general(
            scaled, rows[:, :NS].astype(BF16), (((0,), (0,)), ((), ())), preferred_element_type=F32
        )
        for i in range(group):
            s = group * g + i
            k = where_ref[s + 1]
            product = rows[STEPS * i : STEPS * i + 1, NS + 1 : NS + 2] + rows[STEPS * i : STEPS * i + 1, NS + 2 : NS + 3]
            kept = jnp.where(k >= 0, state[jnp.maximum(k, 0)].astype(F32), 0.0)
            out_state[s] = (kept * product + outer[HEAD * i : HEAD * (i + 1)]).astype(BF16)
        if g % 3 == 2:
            some_rows = pl.ds(group * (g - 2), 3 * group)
            stores.append(
                pltpu.make_async_copy(out_state.at[some_rows], out_hbm.at[some_rows], store_sem.at[g // 3])
            )
            stores[-1].start()
    for store in stores:
        store.wait()


def body(
    hidden,
    ssm_state,
    conv_state,
    lengths,
    dest_owner,
    dest_slot,
    weights_in,
    weights_dt,
    weights_out,
    input_gain,
    conv_weight,
    conv_bias,
    delta_bias,
    decay_log,
    skip_gain,
    output_gain,
):
    shape = jax.ShapeDtypeStruct

    states = ssm_state.reshape(ROWS, HEAD, NS)
    span = shape((ROWS, SPAN), BF16)
    send_state, place, own_weights, square, *spans = pl.pallas_call(
        prepare_kernel,
        name="prepare",
        out_shape=(
            shape((N_ROLL * CAP, HEAD, NS), BF16),
            shape((ROWS,), jnp.int32),
            shape((BLOCK, COLS), BF16),
            shape((ROWS, 1), F32),
            span,
            span,
            span,
            span,
        ),
        in_specs=[SMEM, HBM, HBM, VMEM, VMEM, VMEM, VMEM],
        out_specs=(HBM, SMEM, VMEM, VMEM, HBM, HBM, HBM, HBM),
        scratch_shapes=[
            pltpu.SMEM((N_ROLL,), jnp.int32),
            pltpu.VMEM((ROWS, HEAD, NS), BF16),
            pltpu.VMEM((ROWS, WIDTH), BF16),
            pltpu.SemaphoreType.DMA((2,)),
            pltpu.SemaphoreType.DMA,
            pltpu.SemaphoreType.DMA((4 * NX,)),
        ],
    )(
        dest_owner,
        states,
        hidden,
        input_gain,
        weights_in,
        weights_dt.reshape(1, BLOCK),
        weights_out,
    )
    got_state = lax.all_to_all(
        send_state.reshape(N_ROLL, CAP * HEAD, NS), "roll", split_axis=0, concat_axis=0, tiled=True
    )
    core_perm = [(t, t ^ 1) for t in range(16)]
    z_perm = [
        (t * N_ROLL + z * NY + y, (t ^ 2) * N_ROLL + (NZ - 1 - z) * NY + y)
        for t in range(16)
        for z in range(NZ)
        for y in range(NY)
    ]
    far = lax.ppermute(own_weights, ("train", "roll"), z_perm)
    pair = lax.ppermute(own_weights, "train", core_perm)
    far_pair = lax.ppermute(far, "train", core_perm)

    def x_perm(k):
        return [(t, (t + 4 * k) % 16) for t in range(16)]

    spans = [spans[0]] + [lax.ppermute(spans[k], "train", x_perm(k)) for k in range(1, NX)]
    train = lax.axis_index("train")
    gains = jnp.stack(
        [lax.dynamic_slice_in_dim(input_gain, (train ^ b) * BLOCK, BLOCK) for b in range(4)]
    )
    own, part1, part2, part3 = pl.pallas_call(
        project_kernel,
        name="project",
        out_shape=(shape((ROWS + HEAD, COLS), F32),) + (shape((2 * (ROWS + HEAD), COLS), BF16),) * 3,
        in_specs=[VMEM] * 9,
        out_specs=(VMEM,) * 4,
        cost_estimate=pl.CostEstimate(flops=2 * 256 * SPAN * COLS, bytes_accessed=12000000, transcendentals=0),
    )(gains, *spans, own_weights, pair, far, far_pair)
    parts = [
        lax.ppermute(part, "train", x_perm(NX - k)) for k, part in zip((1, 2, 3), (part1, part2, part3))
    ]

    conv_order = lambda v: jnp.concatenate([v[..., HEAD:], v[..., :HEAD]], axis=-1)
    code = jnp.where(lengths > STEPS, dest_slot + 1, 0).astype(F32)[:, None]
    placeq = (place[None, :] * STEPS + jnp.arange(STEPS, dtype=jnp.int32)[:, None]).reshape(1, -1)
    scalars = jnp.concatenate([delta_bias, decay_log, skip_gain])
    late = pl.pallas_call(
        decode_kernel,
        name="decode",
        out_shape=shape((N_ROLL * CAP * STEPS, LATE), BF16),
        in_specs=[SMEM] + [VMEM] * 5 + [HBM] + [VMEM] * 6,
        out_specs=VMEM,
        scratch_shapes=[
            pltpu.VMEM((ROWS, HEAD, NS), BF16),
            pltpu.VMEM((STEPS * ROWS, LATE), BF16),
            pltpu.SemaphoreType.DMA,
        ],
        cost_estimate=pl.CostEstimate(flops=26_000_000_000, bytes_accessed=40000000, transcendentals=0),
    )(
        scalars,
        own,
        *parts,
        square,
        states,
        conv_order(conv_state.transpose(1, 0, 2)),
        conv_order(conv_weight),
        conv_order(conv_bias)[None],
        output_gain[None],
        code,
        placeq,
    )
    late = pl.pallas_call(
        after_kernel,
        name="after_states",
        out_shape=shape(late.shape, BF16),
        in_specs=[HBM, HBM],
        out_specs=HBM,
        input_output_aliases={0: 0},
    )(late, got_state)
    got_late = lax.all_to_all(
        late.reshape(N_ROLL, CAP * STEPS, LATE), "roll", split_axis=0, concat_axis=0, tiled=True
    ).reshape(N_ROLL * CAP * STEPS, LATE)

    moved_state, moved_conv = pl.pallas_call(
        combine_kernel,
        name="combine",
        out_shape=(shape((ROWS, HEAD, NS), BF16), shape((3, ROWS, CONV), BF16)),
        in_specs=[HBM, VMEM],
        out_specs=(HBM, VMEM),
        scratch_shapes=[
            pltpu.VMEM((N_ROLL * CAP, HEAD, NS), BF16),
            pltpu.VMEM((ROWS, HEAD, NS), BF16),
            pltpu.VMEM((STEPS * ROWS, LATE), F32),
            pltpu.VMEM((8, N_ROLL * CAP * STEPS), jnp.int32),
            pltpu.SMEM((8, N_ROLL * CAP * STEPS), jnp.int32),
            pltpu.SMEM((ROWS + 1,), jnp.int32),
            pltpu.SemaphoreType.DMA,
            pltpu.SemaphoreType.DMA,
            pltpu.SemaphoreType.DMA((4,)),
        ],
    )(got_state.reshape(N_ROLL * CAP, HEAD, NS), got_late)
    return moved_state.reshape(ssm_state.shape), moved_conv.transpose(1, 0, 2)


def solution(mesh):
    rows = ("train", "roll")
    return jax.shard_map(
        body,
        mesh=mesh,
        in_specs=(
            P(rows, None),
            P(rows, None, None, None),
            P(rows, None, None),
            P(rows),
            P(rows),
            P(rows),
            P("train", None),
            P("train", None),
            P(None, "train"),
            P(),
            P(),
            P(),
            P(),
            P(),
            P(),
            P(),
        ),
        out_specs=(P(rows, None, None, None), P(rows, None, None)),
        check_vma=False,
    )
```

```python
import functools

import jax
import jax.numpy as jnp
from jax import lax
from jax.experimental import pallas as pl
from jax.experimental.pallas import tpu as pltpu
from jax.sharding import PartitionSpec as P

STEPS = 4
CAP = 2
ROWS = 48
HEAD = 64
NS = 256
CONV = 576
WIDTH = 8192
NX = 4
NZ = 4
NY = 8
N_ROLL = NZ * NY
BLOCK = 512
SPAN = 4 * BLOCK
COLS = 768
GATE = CONV
BACK = GATE + HEAD
STEP = BACK + HEAD
LATE = NS + CONV + HEAD
F32 = jnp.float32
BF16 = jnp.bfloat16
VMEM = pl.BlockSpec(memory_space=pltpu.VMEM)
SMEM = pl.BlockSpec(memory_space=pltpu.SMEM)
HBM = pl.BlockSpec(memory_space=pltpu.HBM)


def weights_kernel(in_ref, dt_ref, out_ref, weights_ref):
    weights_ref[:, : 2 * NS] = in_ref[:, 2 * HEAD :]
    rest = in_ref[:, : 2 * HEAD].astype(F32)
    weights_ref[:, 2 * NS : BACK] = jnp.concatenate([rest[:, HEAD:], rest[:, :HEAD]], axis=1).astype(BF16)
    steps = jnp.concatenate([dt_ref[...].astype(F32), jnp.zeros((HEAD - 1, BLOCK), F32)], axis=0)
    weights_ref[:, BACK:] = jnp.concatenate([out_ref[...].astype(F32), steps], axis=0).T.astype(BF16)


def prepare_kernel(
    owner_ref,
    state_ref,
    hidden_ref,
    gain_ref,
    send_ref,
    place_ref,
    square_ref,
    h0,
    h1,
    h2,
    h3,
    count_ref,
    states,
    rows,
    load_sem,
    state_sem,
    span_sem,
):
    train = lax.axis_index("train")
    load_rows = pltpu.make_async_copy(hidden_ref, rows, load_sem.at[0])
    load_rows.start()
    load_states = pltpu.make_async_copy(state_ref, states, load_sem.at[1])
    load_states.start()

    load_rows.wait()
    square = jnp.zeros((ROWS, 1), F32)
    for b in range(WIDTH // BLOCK):
        some = rows[:, b * BLOCK : (b + 1) * BLOCK].astype(F32)
        square = square + jnp.sum(some * some, axis=1, keepdims=True)
    square_ref[...] = square
    scale = lax.rsqrt(square * (1.0 / WIDTH) + 1e-05)
    for b in range(WIDTH // BLOCK):
        cols = slice(b * BLOCK, (b + 1) * BLOCK)
        rows[:, cols] = (rows[:, cols].astype(F32) * scale * gain_ref[cols].reshape(1, BLOCK)).astype(BF16)
    spans = []
    for k, ref in enumerate((h0, h1, h2, h3)):
        for b in range(4):
            block = lax.rem(train // 4 + k, NX) * 4 + (lax.rem(train, 4) ^ b)
            spans.append(
                pltpu.make_async_copy(
                    rows.at[:, pl.ds(pl.multiple_of(block * BLOCK, BLOCK), BLOCK)],
                    ref.at[:, pl.ds(b * BLOCK, BLOCK)],
                    span_sem.at[4 * k + b],
                )
            )
            spans[-1].start()
    load_states.wait()
    for o in range(N_ROLL):
        count_ref[o] = 0
    for i in range(ROWS):
        o = owner_ref[i]
        rank = count_ref[o]
        count_ref[o] = rank + 1
        place = o * CAP + rank
        place_ref[i] = place
        pltpu.make_async_copy(states.at[i], send_ref.at[place], state_sem).start()
    pltpu.make_async_copy(states, send_ref.at[pl.ds(0, ROWS)], state_sem).wait()
    for copy in spans:
        copy.wait()


def project_kernel(gain_ref, h0, h1, h2, h3, w0, w1, w2, w3, own_ref, p1, p2, p3):
    count = NX * ROWS
    total, backs = None, None
    for b, w in enumerate((w0, w1, w2, w3)):
        gain = gain_ref[b : b + 1]
        weights = w[...]
        back = weights[:, BACK:].T[:HEAD]
        gained = back.astype(F32) * gain
        high = gained.astype(BF16)
        low = (gained - high.astype(F32)).astype(BF16)
        normed = jnp.concatenate([h[:, b * BLOCK : (b + 1) * BLOCK] for h in (h0, h1, h2, h3)], axis=0)
        left = jnp.concatenate([normed, high, low], axis=0)
        part = jnp.dot(left, weights, preferred_element_type=F32)
        bare = (normed.astype(F32) * (1.0 / gain)).astype(BF16)
        left = jnp.concatenate([bare, back], axis=0)
        part_back = jnp.dot(left, weights[:, BACK:], preferred_element_type=F32)
        total = part if total is None else total + part
        backs = part_back if backs is None else backs + part_back
    total = jnp.concatenate([total[:count], total[count : count + HEAD] + total[count + HEAD :]], axis=0)
    lane = lax.broadcasted_iota(jnp.int32, backs.shape, 1)
    last = jnp.where(lane < HEAD, backs, total[:, BACK:])
    total = jnp.concatenate([total[:, :BACK], last], axis=1)
    grow = total[count:]
    own_ref[:ROWS] = total[:ROWS]
    own_ref[ROWS:] = grow
    grow_high = grow.astype(BF16)
    grow_low = (grow - grow_high.astype(F32)).astype(BF16)
    for k, ref in enumerate((p1, p2, p3)):
        rows = total[(k + 1) * ROWS : (k + 2) * ROWS]
        high = rows.astype(BF16)
        ref[:ROWS] = high
        ref[ROWS : 2 * ROWS] = (rows - high.astype(F32)).astype(BF16)
        ref[2 * ROWS : 2 * ROWS + HEAD] = grow_high
        ref[2 * ROWS + HEAD :] = grow_low


def silu(v):
    return v * jax.nn.sigmoid(v)


def decode_kernel(
    scalar_ref,
    own,
    r1,
    r2,
    r3,
    square_ref,
    state_hbm,
    conv,
    taps,
    bias,
    gain,
    code,
    placeq,
    out,
    state,
    packed,
    state_sem,
):
    load = pltpu.make_async_copy(state_hbm, state, state_sem)
    load.start()
    square = square_ref[...]
    first, grow = own[:ROWS], own[ROWS:]
    for r in (r1, r2, r3):
        first = first + (r[:ROWS].astype(F32) + r[ROWS : 2 * ROWS].astype(F32))
        grow = grow + (r[2 * ROWS : 2 * ROWS + HEAD].astype(F32) + r[2 * ROWS + HEAD :].astype(F32))
    high = grow.astype(BF16)
    grow = jnp.concatenate([high, (grow - high.astype(F32)).astype(BF16)], axis=0)
    raw = first * jnp.sqrt(square * (1.0 / WIDTH) + 1e-05)
    delta_bias, rate, skip = scalar_ref[0], jnp.exp(jnp.full((1, 1), scalar_ref[1], F32)), scalar_ref[2]
    window = [conv[k].astype(F32) for k in range(3)]
    product = jnp.ones((ROWS, 1), F32)
    scaled, inputs_b, entered = [], [], []
    row8 = lax.broadcasted_iota(jnp.int32, (8, HEAD), 0)
    for step in range(STEPS):
        if step == 0:
            projected = first
        else:
            projected = raw * lax.rsqrt(square * (1.0 / WIDTH) + 1e-05)
        conv_input = projected[:, :CONV].astype(BF16).astype(F32)
        window.append(conv_input)
        entered.append(conv_input)
        mixed = bias[...]
        for k in range(4):
            mixed = mixed + window[step + k] * taps[k : k + 1]
        mixed = silu(mixed)
        input_b, output_c, inputs_x = mixed[:, :NS], mixed[:, NS : 2 * NS], mixed[:, 2 * NS :]
        delta = jax.nn.softplus(projected[:, STEP : STEP + 1] + delta_bias)
        decay = jnp.exp(-delta * rate)
        product = product * decay
        scaled = [u * decay for u in scaled] + [delta * inputs_x]
        inputs_b.append(input_b)
        if step == STEPS - 1:
            break
        high = output_c.astype(BF16)
        low = (output_c - high.astype(F32)).astype(BF16)
        if step == 0:
            load.wait()
        reads = []
        for g in range(ROWS // 8):
            left = jnp.concatenate([high[8 * g : 8 * g + 8], low[8 * g : 8 * g + 8]], axis=0)
            acc = jnp.zeros((8, HEAD), F32)
            for half in range(2):
                four = state[8 * g + 4 * half : 8 * g + 4 * half + 4].reshape(4 * HEAD, NS)
                both = lax.dot_general(left, four, (((1,), (1,)), ((), ())), preferred_element_type=F32)
                both = both[:8] + both[8:]
                for i in range(4):
                    acc = jnp.where(row8 == 4 * half + i, both[:, HEAD * i : HEAD * (i + 1)], acc)
            reads.append(acc)
        readout = product * jnp.concatenate(reads, axis=0) + skip * inputs_x
        for u, b in zip(scaled, inputs_b):
            readout = readout + u * jnp.sum(b * output_c, axis=1, keepdims=True)
        gated = readout * silu(projected[:, GATE : GATE + HEAD])
        mean = jnp.mean(gated * gated, axis=1, keepdims=True)
        normed_out = (gated * lax.rsqrt(mean + 1e-05) * gain[...]).astype(BF16)
        twice = jnp.concatenate([normed_out, normed_out], axis=1)
        after = raw + jnp.dot(twice, grow, preferred_element_type=F32)
        cross = raw[:, BACK : BACK + HEAD] + after[:, BACK : BACK + HEAD]
        square = jnp.maximum(
            square + jnp.sum(normed_out.astype(F32) * cross, axis=1, keepdims=True), 0.0
        )
        raw = after
    lane = lax.broadcasted_iota(jnp.int32, (ROWS, CONV), 1)
    high = product.astype(BF16).astype(F32)
    entered[0] = jnp.where(
        lane == 0, code[...], jnp.where(lane == 1, high, jnp.where(lane == 2, product - high, 0.0))
    )
    for step in range(STEPS):
        packed[step * ROWS : (step + 1) * ROWS] = jnp.concatenate(
            [inputs_b[step], entered[step], scaled[step]], axis=1
        ).astype(BF16)
    picker = (
        lax.broadcasted_iota(jnp.int32, (N_ROLL * CAP * STEPS, STEPS * ROWS), 0) == placeq[...]
    ).astype(F32).astype(BF16)
    out[...] = jnp.dot(picker, packed[...], preferred_element_type=F32).astype(BF16)


def after_kernel(late, arrived, out):
    pass


def combine_kernel(
    state_hbm,
    late,
    out_hbm,
    out_conv,
    state,
    out_state,
    rows_ref,
    codes_ref,
    index_ref,
    where_ref,
    sem,
    load_sem,
    store_sem,
):
    load = pltpu.make_async_copy(state_hbm, state, load_sem)
    load.start()
    slots = N_ROLL * CAP
    pick = (lax.broadcasted_iota(jnp.int32, (8, 128), 1) == 0).astype(F32).astype(BF16)
    codes = lax.dot_general(
        pick, late[:, NS : NS + 128], (((1,), (1,)), ((), ())), preferred_element_type=F32
    ).astype(jnp.int32)
    column = lax.broadcasted_iota(jnp.int32, (8, slots * STEPS), 1)
    step_of = column % STEPS
    codes = jnp.where(step_of == 0, codes, 0)
    codes_ref[...] = codes
    copy = pltpu.make_async_copy(codes_ref, index_ref, sem)
    copy.start()
    for step in range(1, STEPS):
        codes = jnp.where(step_of == step, pltpu.roll(codes, 1, axis=1), codes)

    def spread(rows, wanted):
        return (lax.broadcasted_iota(jnp.int32, (rows, slots * STEPS), 0) == wanted[:1]).astype(F32).astype(BF16)

    by_row = jnp.where(codes > 0, (codes - 1) * STEPS + step_of, -1)
    by_step = jnp.where((codes > 0) & (step_of > 0), (step_of - 1) * ROWS + codes - 1, -1)
    rows_ref[...] = jnp.dot(spread(STEPS * ROWS, by_row), late[...], preferred_element_type=F32)
    entered = jnp.dot(
        spread((STEPS - 1) * ROWS, by_step), late[:, NS : NS + CONV], preferred_element_type=F32
    )
    entered = jnp.concatenate([entered[:, 2 * NS :], entered[:, : 2 * NS]], axis=1).astype(BF16)
    for step in range(STEPS - 1):
        out_conv[step] = entered[step * ROWS : (step + 1) * ROWS]
    copy.wait()
    for s in range(ROWS + 1):
        where_ref[s] = -1
    for k in range(slots):
        where_ref[index_ref[0, k * STEPS]] = k

    load.wait()
    stores = []
    group = 4
    lanes = group * HEAD
    some = group * STEPS
    mine = (
        lax.broadcasted_iota(jnp.int32, (some, lanes), 0) // STEPS
        == lax.broadcasted_iota(jnp.int32, (some, lanes), 1) // HEAD
    )
    for g in range(ROWS // group):
        rows = rows_ref[some * g : some * (g + 1)]
        scaled = rows[:, NS + CONV :]
        scaled = jnp.where(mine, jnp.concatenate([scaled] * group, axis=1), 0.0).astype(BF16)
        outer = lax.dot_general(
            scaled, rows[:, :NS].astype(BF16), (((0,), (0,)), ((), ())), preferred_element_type=F32
        )
        for i in range(group):
            s = group * g + i
            k = where_ref[s + 1]
            product = rows[STEPS * i : STEPS * i + 1, NS + 1 : NS + 2] + rows[STEPS * i : STEPS * i + 1, NS + 2 : NS + 3]
            kept = jnp.where(k >= 0, state[jnp.maximum(k, 0)].astype(F32), 0.0)
            out_state[s] = (kept * product + outer[HEAD * i : HEAD * (i + 1)]).astype(BF16)
        if g % 3 == 2:
            some_rows = pl.ds(group * (g - 2), 3 * group)
            stores.append(
                pltpu.make_async_copy(out_state.at[some_rows], out_hbm.at[some_rows], store_sem.at[g // 3])
            )
            stores[-1].start()
    for store in stores:
        store.wait()


def body(
    hidden,
    ssm_state,
    conv_state,
    lengths,
    dest_owner,
    dest_slot,
    weights_in,
    weights_dt,
    weights_out,
    input_gain,
    conv_weight,
    conv_bias,
    delta_bias,
    decay_log,
    skip_gain,
    output_gain,
):
    shape = jax.ShapeDtypeStruct

    states = ssm_state.reshape(ROWS, HEAD, NS)
    span = shape((ROWS, SPAN), BF16)
    own_weights = pl.pallas_call(
        weights_kernel,
        name="pack_weights",
        out_shape=shape((BLOCK, COLS), BF16),
        in_specs=[VMEM] * 3,
        out_specs=VMEM,
    )(weights_in, weights_dt.reshape(1, BLOCK), weights_out)
    send_state, place, square, *spans = pl.pallas_call(
        prepare_kernel,
        name="prepare",
        out_shape=(
            shape((N_ROLL * CAP, HEAD, NS), BF16),
            shape((ROWS,), jnp.int32),
            shape((ROWS, 1), F32),
            span,
            span,
            span,
            span,
        ),
        in_specs=[SMEM, HBM, HBM, VMEM],
        out_specs=(HBM, SMEM, VMEM, HBM, HBM, HBM, HBM),
        scratch_shapes=[
            pltpu.SMEM((N_ROLL,), jnp.int32),
            pltpu.VMEM((ROWS, HEAD, NS), BF16),
            pltpu.VMEM((ROWS, WIDTH), BF16),
            pltpu.SemaphoreType.DMA((2,)),
            pltpu.SemaphoreType.DMA,
            pltpu.SemaphoreType.DMA((4 * NX,)),
        ],
    )(
        dest_owner,
        states,
        hidden,
        input_gain,
    )
    got_state = lax.all_to_all(
        send_state.reshape(N_ROLL, CAP * HEAD, NS), "roll", split_axis=0, concat_axis=0, tiled=True
    )
    core_perm = [(t, t ^ 1) for t in range(16)]
    z_perm = [
        (t * N_ROLL + z * NY + y, (t ^ 2) * N_ROLL + (NZ - 1 - z) * NY + y)
        for t in range(16)
        for z in range(NZ)
        for y in range(NY)
    ]
    far = lax.ppermute(own_weights, ("train", "roll"), z_perm)
    pair = lax.ppermute(own_weights, "train", core_perm)
    far_pair = lax.ppermute(far, "train", core_perm)

    def x_perm(k):
        return [(t, (t + 4 * k) % 16) for t in range(16)]

    spans = [spans[0]] + [lax.ppermute(spans[k], "train", x_perm(k)) for k in range(1, NX)]
    train = lax.axis_index("train")
    gains = jnp.stack(
        [lax.dynamic_slice_in_dim(input_gain, (train ^ b) * BLOCK, BLOCK) for b in range(4)]
    )
    own, part1, part2, part3 = pl.pallas_call(
        project_kernel,
        name="project",
        out_shape=(shape((ROWS + HEAD, COLS), F32),) + (shape((2 * (ROWS + HEAD), COLS), BF16),) * 3,
        in_specs=[VMEM] * 9,
        out_specs=(VMEM,) * 4,
        cost_estimate=pl.CostEstimate(flops=2 * 256 * SPAN * COLS, bytes_accessed=12000000, transcendentals=0),
    )(gains, *spans, own_weights, pair, far, far_pair)
    parts = [
        lax.ppermute(part, "train", x_perm(NX - k)) for k, part in zip((1, 2, 3), (part1, part2, part3))
    ]

    conv_order = lambda v: jnp.concatenate([v[..., HEAD:], v[..., :HEAD]], axis=-1)
    code = jnp.where(lengths > STEPS, dest_slot + 1, 0).astype(F32)[:, None]
    placeq = (place[None, :] * STEPS + jnp.arange(STEPS, dtype=jnp.int32)[:, None]).reshape(1, -1)
    scalars = jnp.concatenate([delta_bias, decay_log, skip_gain])
    late = pl.pallas_call(
        decode_kernel,
        name="decode",
        out_shape=shape((N_ROLL * CAP * STEPS, LATE), BF16),
        in_specs=[SMEM] + [VMEM] * 5 + [HBM] + [VMEM] * 6,
        out_specs=VMEM,
        scratch_shapes=[
            pltpu.VMEM((ROWS, HEAD, NS), BF16),
            pltpu.VMEM((STEPS * ROWS, LATE), BF16),
            pltpu.SemaphoreType.DMA,
        ],
        cost_estimate=pl.CostEstimate(flops=26_000_000_000, bytes_accessed=40000000, transcendentals=0),
    )(
        scalars,
        own,
        *parts,
        square,
        states,
        conv_order(conv_state.transpose(1, 0, 2)),
        conv_order(conv_weight),
        conv_order(conv_bias)[None],
        output_gain[None],
        code,
        placeq,
    )
    late = pl.pallas_call(
        after_kernel,
        name="after_states",
        out_shape=shape(late.shape, BF16),
        in_specs=[HBM, HBM],
        out_specs=HBM,
        input_output_aliases={0: 0},
    )(late, got_state)
    got_late = lax.all_to_all(
        late.reshape(N_ROLL, CAP * STEPS, LATE), "roll", split_axis=0, concat_axis=0, tiled=True
    ).reshape(N_ROLL * CAP * STEPS, LATE)

    moved_state, moved_conv = pl.pallas_call(
        combine_kernel,
        name="combine",
        out_shape=(shape((ROWS, HEAD, NS), BF16), shape((3, ROWS, CONV), BF16)),
        in_specs=[HBM, VMEM],
        out_specs=(HBM, VMEM),
        scratch_shapes=[
            pltpu.VMEM((N_ROLL * CAP, HEAD, NS), BF16),
            pltpu.VMEM((ROWS, HEAD, NS), BF16),
            pltpu.VMEM((STEPS * ROWS, LATE), F32),
            pltpu.VMEM((8, N_ROLL * CAP * STEPS), jnp.int32),
            pltpu.SMEM((8, N_ROLL * CAP * STEPS), jnp.int32),
            pltpu.SMEM((ROWS + 1,), jnp.int32),
            pltpu.SemaphoreType.DMA,
            pltpu.SemaphoreType.DMA,
            pltpu.SemaphoreType.DMA((4,)),
        ],
    )(got_state.reshape(N_ROLL * CAP, HEAD, NS), got_late)
    return moved_state.reshape(ssm_state.shape), moved_conv.transpose(1, 0, 2)


def solution(mesh):
    rows = ("train", "roll")
    return jax.shard_map(
        body,
        mesh=mesh,
        in_specs=(
            P(rows, None),
            P(rows, None, None, None),
            P(rows, None, None),
            P(rows),
            P(rows),
            P(rows),
            P("train", None),
            P("train", None),
            P(None, "train"),
            P(),
            P(),
            P(),
            P(),
            P(),
            P(),
            P(),
        ),
        out_specs=(P(rows, None, None, None), P(rows, None, None)),
        check_vma=False,
    )
```
